32 devices in a mesh: ctx: 8 (over z, y), tp: 4 (over x, core).
Axes of the slice: x: 2, y: 2, z: 4, core: 2. Of those that a mesh axis runs over, the one named last changes fastest.
Arguments:
- query_base: bfloat16 [1024, 3584], P('ctx', 'tp'), may hold values from -6 to 6
- key_base: bfloat16 [1024, 3584], P('ctx', 'tp'), may hold values from -6 to 6
- value_base: bfloat16 [1024, 3584], P('ctx', 'tp'), may hold values from -6 to 6
- adapter_activation: bfloat16 [1024, 128], P('ctx'), may hold values from -6 to 6
- adapter_up_weight: bfloat16 [2, 128, 3584], P(None, None, 'tp'), may hold values from -0.5 to 0.5
- output_grad: bfloat16 [1024, 3584], P('ctx', 'tp'), may hold values from -6 to 6
- stretch_doc: int32 [16], replicated, may hold values from 3 to 15, as said below
- doc_first: int32 [16], replicated, may hold values from 0 to 15, as said below
- slot_stretch: int32 [16], replicated, may hold values from 0 to 15, as said below
Outputs:
- grad_query: bfloat16 [1024, 3584], P('ctx', 'tp')
- grad_key: bfloat16 [1024, 3584], P('ctx', 'tp')
- grad_value: bfloat16 [1024, 3584], P('ctx', 'tp')
- grad_input: bfloat16 [1024, 128], P('ctx')
- grad_adapter: float32 [2, 128, 3584], P(None, None, 'tp')
The draws below stay inside these ranges and needn't reach their ends.
Inputs may be any that keep to these rules, and one draw needn't show every extreme that they name: stretch_doc never falls along the slab; a document covers 1 to 4 consecutive stretches, the first document exactly 4, the last stretch a document of its own; a document's id is the slab index of its last stretch. doc_first[c] is the smallest stretch index with the document id of stretch c. `slot_stretch`: each stretch is held in exactly one slot; slot s lies on ctx index s // 2; the ctx indices of each aligned group of 2 hold exactly that group's 4 consecutive stretches.
All inputs are finite; a program needn't handle non-finite values.
Results may differ from the reference program's by a relative error of at most 0.012.
The reference program's roundings to bfloat16 on the way (of `query`, `value`, `probs_low` and `grad_scores`) count: a program that leaves them out, or rounds other values in their place, can miss the bound.
Values may be sent and summed in bfloat16 or wider, within the bound.
No kernel may reach another device: no remote copies, remote signals or barrier semaphores. Data moves between devices by JAX's collectives and lax.ppermute only.
A program may use at most 64 MiB of HBM per device.

```python
import jax
import jax.numpy as jnp
from jax import lax

LOCAL_HEADS = 16
HEAD_WIDTH = 224
ADAPTER_RANK = 128
STRETCH_LEN = 64
STRETCHES_DEV = 2
GROUP_SIZE = 2
DOC_SPAN = 4
STRETCHES = 16
SLAB_TOKENS = 1024
N_CTX = 8


def documents(key):
    lengths = jax.random.randint(key, (STRETCHES,), 1, DOC_SPAN + 1).astype(jnp.int32)
    lengths = lengths.at[0].set(DOC_SPAN)
    ends = jnp.cumsum(lengths)
    places = jnp.arange(STRETCHES, dtype=jnp.int32)
    owner_doc = jnp.sum((ends[None, :] <= places[:, None]).astype(jnp.int32), axis=1)
    starts = ends - lengths
    first = jnp.sum(jnp.where(places[None, :] == owner_doc[:, None], starts[None, :], 0), axis=1)
    doc_end = jnp.sum(jnp.where(places[None, :] == owner_doc[:, None], ends[None, :], 0), axis=1)
    last_place = STRETCHES - 1
    doc_id = jnp.minimum(doc_end, last_place) - 1
    doc_id = jnp.where(places == last_place, last_place, doc_id)
    first = jnp.where(places == last_place, last_place, first)
    return (doc_id.astype(jnp.int32), first.astype(jnp.int32))


def draw_stretch_doc(key, part):
    return documents(key)[0]


def draw_doc_first(key, part):
    return documents(key)[1]


def draw_slot_stretch(key, part):
    owner_doc, first = documents(key)
    group_stretches = STRETCHES_DEV * GROUP_SIZE
    places = jnp.arange(STRETCHES, dtype=jnp.int32)
    workload = places - first + 1
    priority = (workload * group_stretches + places % group_stretches).reshape(STRETCHES // group_stretches, group_stretches)
    offsets = (jnp.arange(STRETCHES // group_stretches, dtype=jnp.int32) * group_stretches)[:, None]
    ranked = jnp.argsort(priority, axis=1).astype(jnp.int32) + offsets
    lighter = ranked[:, :GROUP_SIZE]
    heavier = ranked[:, ::-1][:, :GROUP_SIZE]
    return jnp.stack([lighter, heavier], axis=2).reshape(STRETCHES).astype(jnp.int32)


def draw_query_base(key, part):
    key = jax.random.fold_in(key, 11)
    values = jnp.clip(jax.random.normal(key, (SLAB_TOKENS, LOCAL_HEADS * HEAD_WIDTH), jnp.float32), -6.0, 6.0)
    return values.astype(jnp.bfloat16)


def draw_key_base(key, part):
    key = jax.random.fold_in(key, 12)
    values = jnp.clip(jax.random.normal(key, (SLAB_TOKENS, LOCAL_HEADS * HEAD_WIDTH), jnp.float32), -6.0, 6.0)
    return values.astype(jnp.bfloat16)


def block_scale(stream_key, extent, pieces, least, largest):
    def one(dim, parts):
        steps = jax.random.uniform(jax.random.fold_in(jax.random.fold_in(stream_key, 6), dim), (parts,), jnp.float32, least / len(pieces), largest / len(pieces))
        return jnp.repeat(jnp.exp(steps), extent[dim] // parts).reshape((-1,) + (1,) * (len(extent) - dim - 1))

    level = one(*pieces[0])
    for cut in pieces[1:]:
        level = level * one(*cut)
    return level


def gaussian(stream_key, shape, deviation, bound, pieces=(), kind=jnp.bfloat16):
    result = deviation * jax.random.normal(stream_key, shape, jnp.float32)
    if pieces:
        result = result * block_scale(stream_key, shape, pieces, -0.22, 0.18)
    return jnp.clip(result, -bound, bound).astype(kind)


def setup_inputs(seed: int = 0) -> dict:
    streams_of = jax.random.split(jax.random.key(seed), 10)
    query_base = draw_query_base(jax.random.fold_in(streams_of[9], 71), 0)
    key_base = draw_key_base(jax.random.fold_in(streams_of[9], 71), 0)
    value_base = gaussian(streams_of[2], (SLAB_TOKENS, LOCAL_HEADS * HEAD_WIDTH), 1.0, 6.0, ((0, 8), (1, 4)))
    adapter_activation = gaussian(streams_of[3], (SLAB_TOKENS, ADAPTER_RANK), 1.0, 6.0, ((0, 8),))
    adapter_up_weight = gaussian(streams_of[4], (2, ADAPTER_RANK, LOCAL_HEADS * HEAD_WIDTH), ADAPTER_RANK ** -0.5, 0.5, ((2, 4),))
    output_grad = gaussian(streams_of[5], (SLAB_TOKENS, LOCAL_HEADS * HEAD_WIDTH), 1.0, 6.0, ((0, 8), (1, 4)))
    stretch_doc = draw_stretch_doc(jax.random.fold_in(streams_of[9], 71), 0)
    doc_first = draw_doc_first(jax.random.fold_in(streams_of[9], 71), 0)
    slot_stretch = draw_slot_stretch(jax.random.fold_in(streams_of[9], 71), 0)
    return {"query_base": query_base, "key_base": key_base, "value_base": value_base, "adapter_activation": adapter_activation, "adapter_up_weight": adapter_up_weight, "output_grad": output_grad, "stretch_doc": stretch_doc, "doc_first": doc_first, "slot_stretch": slot_stretch}


masked_fill = -1e30


def rounded(values):
    return lax.optimization_barrier(values.astype(jnp.bfloat16)).astype(jnp.float32)


def reference(query_base, key_base, value_base, adapter_activation, adapter_up_weight, output_grad, stretch_doc, doc_first, slot_stretch):
    columns = LOCAL_HEADS * HEAD_WIDTH
    block_rows = STRETCHES_DEV * STRETCH_LEN
    window = 2 * DOC_SPAN
    score_scale = HEAD_WIDTH ** -0.5
    query = (query_base.astype(jnp.float32) + jnp.dot(adapter_activation, adapter_up_weight[0], preferred_element_type=jnp.float32)).astype(jnp.bfloat16)
    value = (value_base.astype(jnp.float32) + jnp.dot(adapter_activation, adapter_up_weight[1], preferred_element_type=jnp.float32)).astype(jnp.bfloat16)
    slab_keys = jnp.zeros((STRETCHES, STRETCH_LEN, columns), jnp.bfloat16).at[slot_stretch].set(key_base.reshape(STRETCHES, STRETCH_LEN, columns))
    slab_values = jnp.zeros((STRETCHES, STRETCH_LEN, columns), jnp.bfloat16).at[slot_stretch].set(value.reshape(STRETCHES, STRETCH_LEN, columns))
    front = jnp.zeros((DOC_SPAN, STRETCH_LEN, columns), jnp.bfloat16)
    padded_keys = jnp.concatenate([front, slab_keys], axis=0)
    padded_values = jnp.concatenate([front, slab_values], axis=0)
    padded_doc = jnp.concatenate([jnp.full((DOC_SPAN,), -1, jnp.int32), stretch_doc.astype(jnp.int32)])
    inside = jnp.arange(STRETCH_LEN, dtype=jnp.int32)
    lower = inside[:, None] >= inside[None, :]

    def per_device(carry, device_at):
        key_grads, value_grads = carry
        own = lax.dynamic_slice_in_dim(slot_stretch, device_at * STRETCHES_DEV, STRETCHES_DEV).astype(jnp.int32)
        start = (device_at // GROUP_SIZE) * DOC_SPAN
        window_stretches = start - DOC_SPAN + jnp.arange(window, dtype=jnp.int32)
        window_doc = lax.dynamic_slice_in_dim(padded_doc, start, window)
        own_doc = stretch_doc[own]
        own_first = doc_first[own]
        earlier = (window_stretches[None, :] < own[:, None]) & (window_stretches[None, :] >= own_first[:, None]) & (window_doc[None, :] == own_doc[:, None])
        same = window_stretches[None, :] == own[:, None]
        visible = (earlier[:, None, :, None] | (same[:, None, :, None] & lower[None, :, None, :])).reshape(block_rows, window * STRETCH_LEN)
        key_block = lax.dynamic_slice_in_dim(padded_keys, start, window).reshape(window * STRETCH_LEN, LOCAL_HEADS, HEAD_WIDTH).astype(jnp.float32)
        value_block = lax.dynamic_slice_in_dim(padded_values, start, window).reshape(window * STRETCH_LEN, LOCAL_HEADS, HEAD_WIDTH).astype(jnp.float32)
        query_block = lax.dynamic_slice_in_dim(query, device_at * block_rows, block_rows).reshape(block_rows, LOCAL_HEADS, HEAD_WIDTH).astype(jnp.float32)
        grad_block = lax.dynamic_slice_in_dim(output_grad, device_at * block_rows, block_rows).reshape(block_rows, LOCAL_HEADS, HEAD_WIDTH).astype(jnp.float32)
        scores = jnp.einsum("qhe,khe->hqk", query_block, key_block) * score_scale
        scores = jnp.where(visible[None], scores, masked_fill)
        peak = jnp.max(scores, axis=2, keepdims=True)
        expo = jnp.where(visible[None], jnp.exp(scores - peak), 0.0)
        probs = expo / jnp.sum(expo, axis=2, keepdims=True)
        probs_low = rounded(probs)
        attended = jnp.einsum("hqk,khe->qhe", probs_low, value_block)
        row_dot = jnp.sum(grad_block * attended, axis=2).T
        grad_probs = jnp.einsum("qhe,khe->hqk", grad_block, value_block)
        grad_scores = rounded(probs * (grad_probs - row_dot[..., None]))
        query_gradient = score_scale * jnp.einsum("hqk,khe->qhe", grad_scores, key_block)
        key_terms = score_scale * jnp.einsum("hqk,qhe->khe", grad_scores, query_block)
        value_terms = jnp.einsum("hqk,qhe->khe", probs_low, grad_block)
        mine = jnp.any(window_stretches[:, None] == own[None, :], axis=1)
        mine_rows = jnp.repeat(mine, STRETCH_LEN)[:, None, None]
        key_terms = jnp.where(mine_rows, key_terms, rounded(key_terms)).reshape(window, STRETCH_LEN, columns)
        value_terms = jnp.where(mine_rows, value_terms, rounded(value_terms)).reshape(window, STRETCH_LEN, columns)
        key_grads = lax.dynamic_update_slice_in_dim(key_grads, lax.dynamic_slice_in_dim(key_grads, start, window) + key_terms, start, 0)
        value_grads = lax.dynamic_update_slice_in_dim(value_grads, lax.dynamic_slice_in_dim(value_grads, start, window) + value_terms, start, 0)
        return (key_grads, value_grads), query_gradient.reshape(block_rows, columns)

    grads_init = jnp.zeros((STRETCHES + DOC_SPAN, STRETCH_LEN, columns), jnp.float32)
    (key_grads, value_grads), query_gradient_rows = lax.scan(per_device, (grads_init, grads_init), jnp.arange(N_CTX, dtype=jnp.int32))
    grad_query = query_gradient_rows.reshape(SLAB_TOKENS, columns).astype(jnp.bfloat16)
    grad_key = key_grads[DOC_SPAN:][slot_stretch].reshape(SLAB_TOKENS, columns).astype(jnp.bfloat16)
    grad_value = value_grads[DOC_SPAN:][slot_stretch].reshape(SLAB_TOKENS, columns).astype(jnp.bfloat16)
    grad_input = (jnp.dot(grad_query, adapter_up_weight[0].T, preferred_element_type=jnp.float32) + jnp.dot(grad_value, adapter_up_weight[1].T, preferred_element_type=jnp.float32)).astype(jnp.bfloat16)
    grad_adapter = jnp.stack([jnp.dot(adapter_activation.T, grad_query, preferred_element_type=jnp.float32), jnp.dot(adapter_activation.T, grad_value, preferred_element_type=jnp.float32)])
    return grad_query, grad_key, grad_value, grad_input, grad_adapter
```

```python
import functools

import jax
import jax.numpy as jnp
from jax import lax
from jax.experimental import pallas as pl
from jax.experimental.pallas import tpu as pltpu
from jax.sharding import PartitionSpec as P

HEAD_WIDTH = 224
STRETCHES_DEV = 2
GROUP_SIZE = 2
GROUP_STRETCHES = STRETCHES_DEV * GROUP_SIZE

masked_fill = -1e30
BF16 = jnp.bfloat16
F32 = jnp.float32


def swapped(values):
    half = values.shape[1] // 2
    return jnp.concatenate([values[:, half:], values[:, :half]], axis=1)


def dot(a, b, contract):
    return lax.dot_general(a, b, (contract, ((), ())), preferred_element_type=F32)


def call(kernel, outs, in_smem=0, flops=0):
    def run(*args):
        specs = [
            pl.BlockSpec(memory_space=pltpu.SMEM if i < in_smem else pltpu.VMEM)
            for i in range(len(args))
        ]
        moved = sum(a.size * a.dtype.itemsize for a in (*args, *outs))
        return pl.pallas_call(
            kernel,
            out_shape=outs,
            in_specs=specs,
            out_specs=[pl.BlockSpec(memory_space=pltpu.VMEM) for _ in outs],
            compiler_params=pltpu.CompilerParams(vmem_limit_bytes=40 * 1024 * 1024),
            cost_estimate=pl.CostEstimate(
                flops=flops, bytes_accessed=moved, transcendentals=0
            ),
        )(*args)

    return run


def ctx_at():
    return lax.axis_index("ctx").astype(jnp.int32)


def is_upper():
    return (ctx_at() % GROUP_SIZE) == 1


def is_even():
    return ((ctx_at() // GROUP_SIZE) % 2) == 0


def adapted(base, act, piece):
    update = jnp.dot(act, piece, preferred_element_type=F32)
    return (base.astype(F32) + update).astype(BF16).astype(F32)


def half_of(values, lower):
    half = values.shape[1] // 2
    return jnp.where(lower, values[:, :half], values[:, half:])


def head_of(values, h):
    return values[:, h * HEAD_WIDTH : (h + 1) * HEAD_WIDTH]


def put_pack(out, arrays, h, act=None):
    rows = arrays[0].shape[0]
    stretch_len = rows // STRETCHES_DEV
    pack = jnp.concatenate([head_of(values, h) for values in arrays], axis=1).astype(BF16)
    for s in range(STRETCHES_DEV):
        here = slice(s * stretch_len, (s + 1) * stretch_len)
        out[s, :, : pack.shape[1]] = pack[here]
        if act is not None:
            out[s, :, pack.shape[1] :] = act[here]


def first_kernel(
    k_hbm, v_hbm, q_hbm, g_hbm, a_hbm, w_hbm,
    out, k_ref, v_ref, q_ref, g_ref, a_ref, w_ref, sems,
):
    ends = [
        (a_hbm, a_ref), (w_hbm, w_ref), (v_hbm, v_ref), (q_hbm, q_ref), (k_hbm, k_ref),
        (g_hbm, g_ref),
    ]
    copies = [pltpu.make_async_copy(x, y, sems.at[i]) for i, (x, y) in enumerate(ends)]
    for copy in copies:
        copy.start()
    for copy in copies:
        copy.wait()
    act, lower = a_ref[...], is_upper()
    arrays = (
        k_ref[...].astype(F32),
        adapted(v_ref[...], act, w_ref[1]),
        adapted(q_ref[...], act, w_ref[0]),
        g_ref[...].astype(F32),
    )
    put_pack(out, [half_of(values, lower) for values in arrays], 0, act)


def rest_kernel(
    ctx_count, doc, first, slot, k_ref, v_ref, q_ref, g_ref, a_ref, w_ref,
    sent, own_first, own_second, w_out, places, limits,
):
    act, lower = a_ref[...], is_upper()
    arrays = (
        k_ref[...].astype(F32),
        adapted(v_ref[...], act, w_ref[1]),
        adapted(q_ref[...], act, w_ref[0]),
        g_ref[...].astype(F32),
    )
    put_pack(sent, [half_of(values, lower) for values in arrays], 1)
    mine = [half_of(values, jnp.logical_not(lower)) for values in arrays]
    put_pack(own_first, mine, 0, act)
    put_pack(own_second, mine, 1)
    maps = [half_of(w_ref[i].astype(F32), jnp.logical_not(lower)) for i in range(2)]
    for h in range(2):
        for i in range(2):
            w_out[2 * h + i] = head_of(maps[i], h).astype(BF16)
    put_tables(ctx_count, doc, first, slot, places, limits)


def put_tables(ctx_count, doc, first, slot, places, limits):
    at = ctx_at()
    stretch_len = limits.shape[1] // (GROUP_STRETCHES + 1)
    partner = at + 1 - 2 * (at % GROUP_SIZE)
    has_prev = at >= GROUP_SIZE
    has_next = at < ctx_count - GROUP_SIZE
    base = (at // GROUP_SIZE) * GROUP_STRETCHES
    mine = [
        slot[owner * STRETCHES_DEV + s] for owner in (at, partner) for s in range(STRETCHES_DEV)
    ]
    held = [c % GROUP_STRETCHES for c in mine]
    lanes = lax.broadcasted_iota(jnp.int32, (1, places.shape[1]), 1)
    for row in range(2):
        own = jnp.where(lanes < 2 * HEAD_WIDTH, held[2 * row], held[2 * row + 1])
        places[row : row + 1, :] = own
    four = jnp.where(lanes < 3 * HEAD_WIDTH, held[2], held[3])
    four = jnp.where(lanes < 2 * HEAD_WIDTH, held[1], four)
    places[2:3, :] = jnp.where(lanes < HEAD_WIDTH, held[0], four)
    for j, place in enumerate(held):
        places[3 + j : 4 + j, :] = jnp.full(lanes.shape, place, jnp.int32)
    following = jnp.where(has_next, base + GROUP_STRETCHES, base)
    third = jnp.where(has_prev, base - 2, base)
    fourth = jnp.where(has_prev, base - 1, base)
    left = [(c % GROUP_STRETCHES == 0) & (first[c] < c - 2) for c in mine + [following]]
    queries = [(c, jnp.logical_not(gone)) for c, gone in zip(mine, left)]
    queries.append((following, left[-1] & has_next))
    always = at >= 0
    keys = [(c, always) for c in mine] + [(third, has_prev), (fourth, has_prev)]
    keys.append((following, has_next))
    lanes = lax.broadcasted_iota(jnp.int32, (1, limits.shape[1]), 1)
    for j, (key, there) in enumerate(keys):
        key_doc = doc[key]
        row = jnp.full(lanes.shape, stretch_len, jnp.int32)
        for i, (query, active) in enumerate(queries):
            earlier = (key < query) & (key >= first[query]) & (key_doc == doc[query])
            limit = jnp.where(earlier, -stretch_len, jnp.where(key == query, 0, stretch_len))
            limit = jnp.where(active & there, limit, stretch_len)
            here = (lanes >= i * stretch_len) & (lanes < (i + 1) * stretch_len)
            row = jnp.where(here, limit, row)
        limits[j : j + 1, :] = row


def edge_kernel(places, own, peer, low_out, high_out):
    width = 4 * HEAD_WIDTH
    every = range(STRETCHES_DEV)
    packs = [ref[s].astype(F32) for ref in (own, peer) for s in every]

    def held(place):
        found = packs[0]
        for j in range(1, len(packs)):
            here = places[3 + j : 4 + j, : found.shape[1]] == place
            found = jnp.where(jnp.broadcast_to(here, found.shape), packs[j], found)
        return found

    start, third, fourth = held(0), held(2), held(3)
    pair = 2 * HEAD_WIDTH
    to_next = [third[:, :pair], fourth[:, :pair], third[:, width:], fourth[:, width:]]
    to_prev = [start[:, :width], start[:, width:], start[:, width:]]
    if own.shape[2] == width:
        to_next, to_prev = to_next[:2], to_prev[:1]
    to_next = jnp.concatenate(to_next, axis=1).astype(BF16)
    to_prev = jnp.concatenate(to_prev, axis=1).astype(BF16)
    low_out[...] = jnp.where(is_even(), to_next, to_prev)
    high_out[...] = jnp.where(is_even(), to_prev, to_next)


def attend_kernel(h, limits, own, peer, low_in, high_in, *rest):
    if h == 0:
        act_out, kv_own, kv_peer, dq_out, low_out, high_out, ap_out = rest
    else:
        act_in, low_first, high_first, ap_first = rest[:4]
        kv_own, kv_peer, dq_out, low_out, high_out, ap_out = rest[4:]
    stretch_len = kv_own.shape[0]
    width, pair = 4 * HEAD_WIDTH, 2 * HEAD_WIDTH
    score_scale = HEAD_WIDTH ** (-0.5)
    rows = limits.shape[1]
    inside = lax.broadcasted_iota(jnp.int32, (stretch_len, rows), 1) % stretch_len
    diff = inside - lax.broadcasted_iota(jnp.int32, (stretch_len, rows), 0)
    key_count = GROUP_STRETCHES + 3
    visible = jnp.concatenate([diff >= limits[j : j + 1, :] for j in range(key_count)], axis=0)

    from_next = jnp.where(is_even(), low_in[...], high_in[...])
    from_prev = jnp.where(is_even(), high_in[...], low_in[...])
    packs = [ref[s] for ref in (own, peer) for s in range(STRETCHES_DEV)]
    pairs = packs + [from_prev[:, :pair], from_prev[:, pair:width], from_next]

    def stacked(arrays, i):
        return jnp.concatenate([head_of(values, i) for values in arrays], axis=0)

    key, value = stacked(pairs, 0), stacked(pairs, 1)
    query, grad = stacked(packs + [from_next], 2), stacked(packs + [from_next], 3)
    if h == 0:
        rank = own.shape[2] - width
        acts = [values[:, width:] for values in packs]
        acts += [from_prev[:, width : width + rank], from_prev[:, width + rank :]]
        act = jnp.concatenate(acts + [from_next[:, width : width + rank]], axis=0)
        act_out[...] = act
    else:
        act = act_in[...]
    count = GROUP_STRETCHES * stretch_len
    act_query = jnp.concatenate([act[:count], act[-stretch_len:]], axis=0)

    scores = jnp.where(visible, dot(key, query, ((1,), (1,))) * score_scale, masked_fill)
    peak = jnp.max(scores, axis=0, keepdims=True)
    expo = jnp.where(visible, jnp.exp(scores - peak), 0.0)
    norm_sum = jnp.maximum(jnp.sum(expo, axis=0, keepdims=True), 1.0)
    probs = expo / norm_sum
    probs_low = probs.astype(BF16)
    grad_probs = dot(value, grad, ((1,), (1,)))
    row_dot = jnp.sum(probs_low.astype(F32) * grad_probs, axis=0, keepdims=True)
    grad_scores = (probs * (grad_probs - row_dot)).astype(BF16)
    dq = dot(grad_scores, key, ((0,), (0,))) * score_scale
    dk = dot(grad_scores, query, ((1,), (0,))) * score_scale
    dv = dot(probs_low, grad, ((1,), (0,)))
    ap_q = dot(act_query, dq.astype(BF16), ((0,), (0,)))
    ap_v = dot(act, dv.astype(BF16), ((0,), (0,)))

    def beside(*parts):
        return jnp.concatenate(
            [values[i * stretch_len : (i + 1) * stretch_len] for values, i in parts], axis=1
        )

    to_prev = beside((dk, 4), (dv, 4), (dk, 5), (dv, 5)).astype(BF16)
    to_next = beside((dk, 6), (dv, 6), (dq, 4), (dq, 4)).astype(BF16)
    low_back = jnp.where(is_even(), to_next, to_prev)
    high_back = jnp.where(is_even(), to_prev, to_next)
    kv_own[...] = beside((dk, 0), (dv, 0), (dk, 1), (dv, 1))
    kv_peer[...] = beside((dk, 2), (dv, 2), (dk, 3), (dv, 3))
    dq_out[...] = beside((dq, 0), (dq, 1), (dq, 2), (dq, 3)).astype(BF16)
    ap = beside((ap_q, 0), (ap_v, 0), (ap_q, 1), (ap_v, 1))
    if h == 0:
        low_out[...], high_out[...], ap_out[...] = low_back, high_back, ap
        return
    high_out[:, :width] = high_first[...]
    high_out[:, width:] = high_back
    low_out[:, :width] = low_first[...]
    low_out[:, width : 2 * width] = low_back
    low_out[:, 2 * width :] = jnp.where(is_even(), ap, ap_first[...]).astype(BF16)
    ap_out[...] = jnp.where(is_even(), ap_first[...], ap)


def put_totals(row, places, kvs, dqs, high_in, low_in, out):
    width, pair = 4 * HEAD_WIDTH, 2 * HEAD_WIDTH
    for h, (kv, dq) in enumerate(zip(kvs, dqs)):
        here = slice(h * width, (h + 1) * width)
        from_next = jnp.where(is_even(), low_in[:, here], high_in[:, here]).astype(F32)
        from_prev = jnp.where(is_even(), high_in[:, here], low_in[:, here]).astype(F32)
        low = lax.broadcasted_iota(jnp.int32, from_next.shape, 1) < pair
        next_swapped = swapped(from_next)
        third = jnp.where(low, from_next, next_swapped)
        fourth = jnp.where(low, next_swapped, from_next)
        start = jnp.where(low, from_prev, swapped(from_prev))
        place = jnp.broadcast_to(places[row : row + 1, :width], kv.shape)
        back = jnp.where(place == 2, third, jnp.where(place == 3, fourth, 0.0))
        back = jnp.where(place == 0, start, back)
        at = h * (width + pair)
        out[:, at : at + width] = (kv[...] + back).astype(BF16)
        query_back = head_of(from_prev, 2)
        query_back = jnp.concatenate([query_back, query_back], axis=1)
        place = places[2:3, row * pair : (row + 1) * pair]
        place = jnp.broadcast_to(place, query_back.shape)
        mine = dq[:, row * pair : (row + 1) * pair].astype(F32)
        total = mine + jnp.where(place == 0, query_back, 0.0)
        out[:, at + width : at + width + pair] = total.astype(BF16)


def input_part(packs, w_ref):
    parts = []
    for h in range(2):
        pack = packs[:, h * 6 * HEAD_WIDTH : (h + 1) * 6 * HEAD_WIDTH]
        values = jnp.concatenate([head_of(pack, 1), head_of(pack, 3)], axis=0)
        queries = jnp.concatenate([head_of(pack, 4), head_of(pack, 5)], axis=0)
        parts.append(dot(queries, w_ref[2 * h], ((1,), (1,))))
        parts.append(dot(values, w_ref[2 * h + 1], ((1,), (1,))))
    return sum(parts)


def peer_totals_kernel(
    places, kv_first, kv_second, dq_first, dq_second, high_in, low_in, send
):
    put_totals(1, places, (kv_first, kv_second), (dq_first, dq_second), high_in, low_in, send)


def own_totals_kernel(
    places, kv_first, kv_second, dq_first, dq_second, ap_keep, w_ref, send, high_in, low_in,
    keep, part, peer_part, ap_sum,
):
    ap_sum[...] = (ap_keep[...] + low_in[:, 8 * HEAD_WIDTH :].astype(F32)).astype(BF16)
    put_totals(0, places, (kv_first, kv_second), (dq_first, dq_second), high_in, low_in, keep)
    part[...] = input_part(keep, w_ref)
    peer_part[...] = input_part(send, w_ref).astype(BF16)


def all_heads(mine, theirs):
    upper = is_upper()
    mine, theirs = ([values.astype(F32) for values in side] for side in (mine, theirs))
    lower_heads = [jnp.where(upper, b, a) for a, b in zip(mine, theirs)]
    return lower_heads + [jnp.where(upper, a, b) for a, b in zip(mine, theirs)]


def heads_beside(packs, i):
    return jnp.concatenate([head_of(values, i) for values in packs], axis=1)


def grads_out_kernel(keep, recv, grad_query, grad_key, grad_value, done):
    stretch_len = keep.shape[0]
    wide = 6 * HEAD_WIDTH
    every = [slice(h * wide, (h + 1) * wide) for h in range(2)]
    packs = all_heads([keep[:, here] for here in every], [recv[:, here] for here in every])
    for s in range(STRETCHES_DEV):
        here = slice(s * stretch_len, (s + 1) * stretch_len)
        grad_key[here, :] = heads_beside(packs, 2 * s).astype(BF16)
        grad_value[here, :] = heads_beside(packs, 2 * s + 1).astype(BF16)
        grad_query[here, :] = heads_beside(packs, 4 + s).astype(BF16)
    done[...] = jnp.zeros(done.shape, done.dtype)


def adapter_out_kernel(own, peer_other, other, peer_own, input_sum, awaited, out, grad_input):
    even = is_even()
    rows = out.shape[1] // 2
    grad_input[...] = input_sum[...].astype(BF16)
    own, other, peer_own, peer_other = (
        ref[...].astype(F32) for ref in (own, other, peer_own, peer_other)
    )
    packs = all_heads(
        (jnp.where(even, own, other), jnp.where(even, other, own)),
        (jnp.where(even, peer_own, peer_other), jnp.where(even, peer_other, peer_own)),
    )
    for w in range(2):
        for i in range(2):
            out[w, i * rows : (i + 1) * rows, :] = heads_beside(packs, 2 * i + w)


def body(
    query_base, key_base, value_base, adapter_activation, adapter_up_weight, output_grad,
    stretch_doc, doc_first, slot_stretch,
):
    row_count, columns = query_base.shape
    rank = adapter_activation.shape[1]
    stretch_len = row_count // STRETCHES_DEV
    width = 4 * HEAD_WIDTH
    ctx_count = lax.axis_size("ctx")
    tp_count = lax.axis_size("tp")
    groups = ctx_count // GROUP_SIZE
    shape = jax.ShapeDtypeStruct

    def exchanged(array, flip):
        return lax.ppermute(array, "ctx", [(i, i ^ flip) for i in range(ctx_count)])

    def with_odd_pairs(array):
        pairs = []
        for i in range(ctx_count):
            group = i // GROUP_SIZE
            other = group + 1 if group % 2 else group - 1
            for t in range(tp_count):
                to = (i, t ^ 1)
                if 0 <= other < groups:
                    to = (other * GROUP_SIZE + i % GROUP_SIZE, t)
                pairs.append((i * tp_count + t, to[0] * tp_count + to[1]))
        return lax.ppermute(array, ("ctx", "tp"), pairs)

    def first_pack(*args):
        anywhere = pl.BlockSpec(memory_space=pl.ANY)
        return pl.pallas_call(
            first_kernel,
            out_shape=shape((STRETCHES_DEV, stretch_len, width + rank), BF16),
            in_specs=[anywhere] * len(args),
            out_specs=pl.BlockSpec(memory_space=pltpu.VMEM),
            scratch_shapes=[pltpu.VMEM(a.shape, a.dtype) for a in args]
            + [pltpu.SemaphoreType.DMA((len(args),))],
        )(*args)

    arrays = (
        key_base, value_base, query_base, output_grad, adapter_activation, adapter_up_weight
    )
    peer_first = exchanged(first_pack(*arrays), 1)
    pack_first = shape((STRETCHES_DEV, stretch_len, width + rank), BF16)
    pack_second = shape((STRETCHES_DEV, stretch_len, width), BF16)
    outs = [
        pack_second,
        pack_first,
        pack_second,
        shape((4, rank, HEAD_WIDTH), BF16),
        shape((3 + GROUP_STRETCHES, width + rank), jnp.int32),
        shape((GROUP_STRETCHES + 3, (GROUP_STRETCHES + 1) * stretch_len), jnp.int32),
    ]
    sent, own_first, own_second, w_heads, places, limits = call(
        functools.partial(rest_kernel, ctx_count), outs, 3
    )(stretch_doc, doc_first, slot_stretch, *arrays)

    peer_second = exchanged(sent, 1)
    edge = shape((stretch_len, width + 2 * rank), BF16)
    low_sent, high_sent = call(edge_kernel, [edge] * 2)(places, own_first, peer_first)
    high_first = with_odd_pairs(high_sent)
    low_first = exchanged(low_sent, GROUP_SIZE)
    edge = shape((stretch_len, width), BF16)
    low_sent, high_sent = call(edge_kernel, [edge] * 2)(places, own_second, peer_second)
    high_second = with_odd_pairs(high_sent)
    low_second = exchanged(low_sent, GROUP_SIZE)

    wide, low = shape((stretch_len, width), F32), shape((stretch_len, width), BF16)
    outs = [wide, wide, low, low, low, wide]
    act_rows = (GROUP_STRETCHES + 3) * stretch_len
    act, kv_own_first, kv_peer_first, dq_first, low_back, high_back, ap_first = call(
        functools.partial(attend_kernel, 0), [shape((act_rows, rank), BF16)] + outs
    )(limits, own_first, peer_first, low_first, high_first)
    outs = [wide, wide, low, shape((stretch_len, 3 * width), BF16)]
    outs += [shape((stretch_len, 2 * width), BF16), wide]
    kv_own_second, kv_peer_second, dq_second, low_back, high_back, ap_keep = call(
        functools.partial(attend_kernel, 1), outs
    )(
        limits, own_second, peer_second, low_second, high_second,
        act, low_back, high_back, ap_first,
    )
    low_back = exchanged(low_back, GROUP_SIZE)
    high_back = with_odd_pairs(high_back)

    back = shape((stretch_len, 2 * (width + 2 * HEAD_WIDTH)), BF16)
    (send,) = call(peer_totals_kernel, [back])(
        places, kv_peer_first, kv_peer_second, dq_first, dq_second, high_back, low_back
    )
    recv = exchanged(send, 1)
    part_dims = (row_count, rank)
    outs = [back, shape(part_dims, F32), shape(part_dims, BF16), low]
    keep, own_part, peer_part, total = call(own_totals_kernel, outs)(
        places, kv_own_first, kv_own_second, dq_first, dq_second, ap_keep, w_heads, send,
        high_back, low_back,
    )
    gi_recv = exchanged(peer_part, 1)

    flip = 2
    while flip < groups:
        theirs = exchanged(total, flip * GROUP_SIZE)
        total = (total.astype(F32) + theirs.astype(F32)).astype(BF16)
        flip *= 2
    peer_total = exchanged(total, 1)
    other = exchanged(total, GROUP_SIZE)
    peer_other = exchanged(total, GROUP_SIZE + 1)

    part = (own_part + gi_recv.astype(F32)).astype(BF16)
    sums = [part.astype(F32)]
    for by in range(1, tp_count):
        pairs = [(i, i ^ by) for i in range(tp_count)]
        sums.append(lax.ppermute(part, "tp", pairs).astype(F32))
    while len(sums) > 1:
        sums = [a + b for a, b in zip(sums[::2], sums[1::2])]

    outs = [shape((row_count, columns), BF16)] * 3 + [shape((8, 128), F32)]
    grad_query, grad_key, grad_value, done = call(grads_out_kernel, outs)(keep, recv)
    outs = [shape((2, rank, columns), F32), shape((row_count, rank), BF16)]
    grad_adapter, grad_input = call(adapter_out_kernel, outs)(
        total, peer_other, other, peer_total, sums[0], done
    )
    return (grad_query, grad_key, grad_value, grad_input, grad_adapter)


def solution(mesh):
    return jax.shard_map(
        body,
        mesh=mesh,
        in_specs=(
            P("ctx", "tp"),
            P("ctx", "tp"),
            P("ctx", "tp"),
            P("ctx", None),
            P(None, None, "tp"),
            P("ctx", "tp"),
            P(),
            P(),
            P(),
        ),
        out_specs=(
            P("ctx", "tp"),
            P("ctx", "tp"),
            P("ctx", "tp"),
            P("ctx", None),
            P(None, None, "tp"),
        ),
        check_vma=False,
    )
```
